128 devices in a mesh: row: 16 (over x, z), col: 8 (over y, core).
Axes of the slice: x: 4, y: 4, z: 4, core: 2. Of those that a mesh axis runs over, the one named last changes fastest.
Arguments:
- phi_modes: bfloat16 [1536, 1024, 512], P(('row', 'col')), may hold values from -6 to 6
- trace_maps: bfloat16 [1536, 256, 1024], P(('row', 'col')), may hold values from -0.1875 to 0.1875
- mortar: bfloat16 [1024, 256, 256], P(('row', 'col')), may hold values from -0.0234375 to 0.0234375
- pair_list: int32 [1024, 2], P(('row', 'col')), may hold values from 0 to 1535, as said below
- iface_counts: int32 [1024], P(('row', 'col')), may hold values from 64 to 256
Outputs:
- coupling: bfloat16 [1024, 512, 512], P(('row', 'col'))
The draws below stay inside these ranges and needn't reach their ends.
Inputs may be any that keep to these rules, and one draw needn't show every extreme that they name: Substructure s belongs to device s // 12, devices numbered row-major over (row, col). Row p of pair_list lies on the device that owns its i; its j is owned by that device or by a neighbouring device one step along row (no wrap) or along col (cyclic). Of one device's 8 pairs at most 2 have j on any one other device, and that many do in every draw; every existing neighbouring device owns the j of some pair of the device.
All inputs are finite; a program needn't handle non-finite values.
Results may differ from the reference program's by a relative error of at most 0.0064.
Values may be sent and summed in bfloat16 or wider, within the bound.
A program may use at most 128 MiB of HBM per device.

```python
import jax
import jax.numpy as jnp
from jax import lax

MODES = 512
BOUNDARY_DOF = 1024
IFACE_DOF = 256
SUB_DEV = 12
PAIR_DEV = 8
DIR_CAP = 2
SUBS = 1536
PAIRS = 1024
N_ROW = 16
N_COL = 8
DEVICES = 128


def draw_pair_list(key, part):
    key = jax.random.fold_in(key, 7)
    k_dirs, k_slots, k_first, k_second = jax.random.split(key, 4)
    device = jnp.arange(DEVICES, dtype=jnp.int32)
    row_pos = device // N_COL
    col_pos = device % N_COL
    orders = jax.vmap(lambda k: jax.random.permutation(k, 4))(jax.random.split(k_dirs, DEVICES)).astype(jnp.int32) + 1
    labels = jnp.concatenate([orders, jnp.zeros((DEVICES, 1), jnp.int32)], 1)
    slot = jnp.arange(PAIR_DEV, dtype=jnp.int32)
    pattern = jnp.where(slot < DIR_CAP, 0, 1 + (slot - DIR_CAP) % 4).astype(jnp.int32)
    shuffled = jax.vmap(lambda k: jax.random.permutation(k, PAIR_DEV))(jax.random.split(k_slots, DEVICES))
    chosen = jnp.take_along_axis(labels, pattern[shuffled], axis=1)
    edge = (chosen == 1) & (row_pos[:, None] == 0) | (chosen == 2) & (row_pos[:, None] == N_ROW - 1)
    chosen = jnp.where(edge, 0, chosen)
    target_row = row_pos[:, None] + jnp.where(chosen == 1, -1, 0) + jnp.where(chosen == 2, 1, 0)
    target_col = (col_pos[:, None] + jnp.where(chosen == 3, -1, 0) + jnp.where(chosen == 4, 1, 0)) % N_COL
    target = target_row * N_COL + target_col
    first = device[:, None] * SUB_DEV + jax.random.randint(k_first, (DEVICES, PAIR_DEV), 0, SUB_DEV)
    second = target * SUB_DEV + jax.random.randint(k_second, (DEVICES, PAIR_DEV), 0, SUB_DEV)
    return jnp.stack([first, second], -1).reshape(PAIRS, 2).astype(jnp.int32)


def with_ends(array, rng, smallest, top_value):
    place = [jax.random.randint(jax.random.fold_in(rng, axis), (), 0, length) for axis, length in enumerate(array.shape)]
    longest = array.shape.index(max(array.shape))
    beside = place[:longest] + [(place[longest] + 1) % array.shape[longest]] + place[longest + 1:]
    return array.at[tuple(place)].set(smallest).at[tuple(beside)].set(top_value)


def block_levels(stream_key, extent, cuts, low, largest):
    level, own = 1.0, jax.random.fold_in(stream_key, 6)
    for axis_at, parts in cuts:
        steps = jnp.exp(jax.random.uniform(jax.random.fold_in(own, axis_at), (parts,), jnp.float32, low / len(cuts), largest / len(cuts)))
        level = level * jnp.repeat(steps, extent[axis_at] // parts).reshape([-1 if axis == axis_at else 1 for axis in range(len(extent))])
    return level


def scatter_about(stream_key, extent, scale, bound, cuts=(), held_as=jnp.bfloat16):
    factor_of = block_levels(stream_key, extent, cuts, -0.22, 0.18) if cuts else 1.0
    values = jax.random.normal(stream_key, extent, jnp.float32) * scale * factor_of
    return jnp.minimum(jnp.maximum(values, -bound), bound).astype(held_as)


def setup_inputs(seed: int = 0) -> dict:
    streams_of = jax.random.split(jax.random.key(seed), 6)
    return {
        "phi_modes": scatter_about(streams_of[0], (SUBS, BOUNDARY_DOF, MODES), 1.0, 6.0, ((0, 128),)),
        "trace_maps": scatter_about(streams_of[1], (SUBS, IFACE_DOF, BOUNDARY_DOF), BOUNDARY_DOF ** -0.5, 0.1875, ((0, 128),)),
        "mortar": scatter_about(streams_of[2], (PAIRS, IFACE_DOF, IFACE_DOF), (IFACE_DOF * IFACE_DOF) ** -0.5, 0.0234375, ((0, 128),)),
        "pair_list": draw_pair_list(jax.random.fold_in(streams_of[5], 71), 0),
        "iface_counts": with_ends(jax.random.randint(streams_of[4], (PAIRS,), IFACE_DOF // 4, IFACE_DOF + 1), jax.random.fold_in(streams_of[4], 1), IFACE_DOF // 4, IFACE_DOF).astype(jnp.int32),
    }


def reference(phi_modes, trace_maps, mortar, pair_list, iface_counts):
    def project(block):
        maps, modes = block
        return jnp.einsum("snb,sbk->snk", maps.astype(jnp.float32), modes.astype(jnp.float32)).astype(jnp.bfloat16)

    panels = lax.map(project, (trace_maps.reshape(DEVICES, SUB_DEV, IFACE_DOF, BOUNDARY_DOF),
                               phi_modes.reshape(DEVICES, SUB_DEV, BOUNDARY_DOF, MODES)))
    panels = panels.reshape(SUBS, IFACE_DOF, MODES)

    def couple(block):
        panel_block, pairs, counts = block
        own = panels[pairs[:, 0]].astype(jnp.float32)
        partner = panels[pairs[:, 1]].astype(jnp.float32)
        inside = jnp.arange(IFACE_DOF, dtype=jnp.int32)[None, :] < counts[:, None]
        keep = (inside[:, :, None] & inside[:, None, :]).astype(jnp.float32)
        masked = panel_block.astype(jnp.float32) * keep
        applied = jnp.einsum("pnm,pmk->pnk", masked, partner).astype(jnp.bfloat16)
        return jnp.einsum("pnk,pnl->pkl", own, applied.astype(jnp.float32)).astype(jnp.bfloat16)

    result = lax.map(couple, (mortar.reshape(DEVICES, PAIR_DEV, IFACE_DOF, IFACE_DOF),
                              pair_list.reshape(DEVICES, PAIR_DEV, 2),
                              iface_counts.reshape(DEVICES, PAIR_DEV)))
    return result.reshape(PAIRS, MODES, MODES)
```

```python
import functools

import jax
import jax.numpy as jnp
from jax import lax
from jax.experimental import pallas as pl
from jax.experimental.pallas import tpu as pltpu
from jax.sharding import PartitionSpec as P

MESH = pl.DeviceIdType.MESH
WIDTH = 256
CAP = 2


def panels_kernel(
    nrow,
    ncol,
    phi_hbm,
    trace_hbm,
    mortar_hbm,
    pairs,
    counts,
    panels,
    arrived,
    left,
    route,
    phi,
    trace,
    mortar,
    outgoing,
    wanted,
    asked,
    phi_sem,
    trace_sem,
    mortar_sem,
    ask_send,
    ask_recv,
    send_sem,
    recv_sem,
):
    parts, owned, iface, width = panels.shape
    npair = mortar.shape[0]
    row = lax.axis_index("row")
    col = lax.axis_index("col")
    mine = row * ncol + col
    near = [
        (lax.rem(row + nrow - 1, nrow), col),
        (lax.rem(row + 1, nrow), col),
        (row, lax.rem(col + ncol - 1, ncol)),
        (row, lax.rem(col + 1, ncol)),
    ]

    barrier = pltpu.get_barrier_semaphore()
    for device in near:
        pl.semaphore_signal(barrier, inc=1, device_id=device, device_id_type=MESH)

    def trace_copy(s):
        return pltpu.make_async_copy(trace_hbm.at[s], trace.at[s], trace_sem.at[s])

    def phi_copy(c, s):
        return pltpu.make_async_copy(
            phi_hbm.at[s, :, pl.ds(c * width, width)], phi.at[c, s], phi_sem.at[c, s]
        )

    mortar_copy = pltpu.make_async_copy(mortar_hbm, mortar, mortar_sem)

    @pl.loop(0, owned)
    def _(s):
        trace_copy(s).start()
        phi_copy(0, s).start()

    for c in range(1, parts):
        @pl.loop(0, owned)
        def _(s):
            phi_copy(c, s).start()

    mortar_copy.start()

    base = [(r * ncol + k) * owned for r, k in near]
    taken = [jnp.int32(0)] * 4
    first = [jnp.int32(0)] * 4
    second = [jnp.int32(0)] * 4
    for p in range(npair):
        j = pairs[1, p]
        place = jnp.clip(j - mine * owned, 0, owned - 1)
        for d in range(4):
            local = j - base[d]
            hit = (local >= 0) & (local < owned)
            first[d] = jnp.where(hit & (taken[d] == 0), local, first[d])
            second[d] = jnp.where(hit & (taken[d] == 1), local, second[d])
            place = jnp.where(hit, owned + CAP * d + jnp.minimum(taken[d], CAP - 1), place)
            taken[d] = taken[d] + hit.astype(jnp.int32)
        route[p] = place
    for d in range(4):
        wanted[d, 0] = first[d]
        wanted[d, 1] = second[d]

    pl.semaphore_wait(barrier, 4)
    asks = [
        pltpu.make_async_remote_copy(
            src_ref=wanted.at[d],
            dst_ref=asked.at[d ^ 1],
            send_sem=ask_send.at[d],
            recv_sem=ask_recv.at[d ^ 1],
            device_id=near[d],
            device_id_type=MESH,
        )
        for d in range(4)
    ]
    for ask in asks:
        ask.start()

    sends = []
    for c in range(parts):
        @pl.loop(0, owned)
        def _(s):
            if c == 0:
                trace_copy(s).wait()
            phi_copy(c, s).wait()
            panels[c, s] = jnp.dot(
                trace[s], phi[c, s], preferred_element_type=jnp.float32
            ).astype(panels.dtype)

        if c == 0:
            for ask in asks:
                ask.wait()
        for d in range(4):
            for k in range(CAP):
                outgoing[c, d, k] = panels[c, asked[d, k]]
            send = pltpu.make_async_remote_copy(
                src_ref=outgoing.at[c, d],
                dst_ref=arrived.at[c, d ^ 1],
                send_sem=send_sem.at[c, d],
                recv_sem=recv_sem.at[c, d ^ 1],
                device_id=near[d],
                device_id_type=MESH,
            )
            send.start()
            sends.append(send)

    mortar_copy.wait()
    rows = lax.broadcasted_iota(jnp.int32, (iface, iface), 0)
    columns = lax.broadcasted_iota(jnp.int32, (iface, iface), 1)

    @pl.loop(0, npair)
    def _(p):
        own = jnp.clip(pairs[0, p] - mine * owned, 0, owned - 1)
        count = counts[p]
        keep = (rows < count) & (columns < count)
        masked = jnp.where(keep, mortar[p].astype(jnp.float32), 0.0).astype(mortar.dtype)
        for c in range(parts):
            left[p, pl.ds(c * width, width), :] = lax.dot_general(
                panels[c, own],
                masked,
                (((0,), (0,)), ((), ())),
                preferred_element_type=jnp.float32,
            ).astype(left.dtype)

    for send in sends:
        send.wait()


def coupling_kernel(route, panels, arrived, left, coupling):
    parts, owned, iface, width = panels.shape
    p = pl.program_id(0)
    place = route[p]

    def multiply(partner):
        for c in range(parts):
            coupling[0, :, pl.ds(c * width, width)] = jnp.dot(
                left[p], partner(c), preferred_element_type=jnp.float32
            ).astype(coupling.dtype)

    @pl.when(place < owned)
    def _():
        multiply(lambda c: panels[c, place])

    @pl.when(place >= owned)
    def _():
        multiply(lambda c: arrived[c, (place - owned) // CAP, (place - owned) % CAP])


def body(nrow, ncol, phi_modes, trace_maps, mortar, pair_list, iface_counts):
    owned, boundary, modes = phi_modes.shape
    npair, iface, _ = mortar.shape
    parts = modes // WIDTH
    dtype = phi_modes.dtype
    hbm = pl.BlockSpec(memory_space=pltpu.HBM)
    smem = pl.BlockSpec(memory_space=pltpu.SMEM)
    vmem = pl.BlockSpec(memory_space=pltpu.VMEM)
    dma = pltpu.SemaphoreType.DMA
    panels, arrived, left, route = pl.pallas_call(
        functools.partial(panels_kernel, nrow, ncol),
        out_shape=(
            pltpu.VMEM((parts, owned, iface, WIDTH), dtype),
            pltpu.VMEM((parts, 4, CAP, iface, WIDTH), dtype),
            pltpu.VMEM((npair, modes, iface), dtype),
            pltpu.SMEM((npair,), jnp.int32),
        ),
        in_specs=[hbm, hbm, hbm, smem, smem],
        out_specs=(vmem, vmem, vmem, smem),
        scratch_shapes=[
            pltpu.VMEM((parts, owned, boundary, WIDTH), dtype),
            pltpu.VMEM((owned, iface, boundary), dtype),
            pltpu.VMEM((npair, iface, iface), dtype),
            pltpu.VMEM((parts, 4, CAP, iface, WIDTH), dtype),
            pltpu.SMEM((4, 128), jnp.int32),
            pltpu.SMEM((4, 128), jnp.int32),
            dma((parts, owned)),
            dma((owned,)),
            dma,
            dma((4,)),
            dma((4,)),
            dma((parts, 4)),
            dma((parts, 4)),
        ],
        compiler_params=pltpu.CompilerParams(
            collective_id=0, has_side_effects=True, vmem_limit_bytes=48 * 2**20
        ),
        name="panels",
    )(phi_modes, trace_maps, mortar, pair_list.T, iface_counts)
    return pl.pallas_call(
        coupling_kernel,
        out_shape=jax.ShapeDtypeStruct((npair, modes, modes), dtype),
        grid=(npair,),
        in_specs=[smem, vmem, vmem, vmem],
        out_specs=pl.BlockSpec((1, modes, modes), lambda p: (p, 0, 0)),
        compiler_params=pltpu.CompilerParams(vmem_limit_bytes=32 * 2**20),
        name="coupling",
    )(route, panels, arrived, left)


def solution(mesh):
    return jax.shard_map(
        functools.partial(body, mesh.shape["row"], mesh.shape["col"]),
        mesh=mesh,
        in_specs=(
            P(("row", "col"), None, None),
            P(("row", "col"), None, None),
            P(("row", "col"), None, None),
            P(("row", "col"), None),
            P(("row", "col")),
        ),
        out_specs=P(("row", "col"), None, None),
        check_vma=False,
    )
```

```python
import functools

import jax
import jax.numpy as jnp
from jax import lax
from jax.experimental import pallas as pl
from jax.experimental.pallas import tpu as pltpu
from jax.sharding import PartitionSpec as P

MESH = pl.DeviceIdType.MESH
ROW_STEPS = (1, 0)
COLUMN_STEPS = (2, 3)
CAP = 2
ROW_BLOCKS = ((0, 128), (128, 128))
COLUMN_BLOCKS = ((0, 256), (256, 256))
PIECES = (((0,), (0,)), ((1,), (0,)), ((0, 1), (1,)))
GROUP = 4


def extent(blocks, chosen):
    return sum(blocks[b][1] for b in chosen)


def panels_kernel(nrow, ncol, *refs):
    refs = list(refs)

    def take(count):
        taken = refs[:count]
        del refs[:count]
        return taken

    phi_hbm, trace_hbm, mortar_hbm, pairs_hbm, counts_hbm = take(5)
    panels, left, route, across = take(4)
    arrived = take(len(PIECES))
    phi = take(len(COLUMN_BLOCKS))
    trace = take(len(ROW_BLOCKS))
    outgoing = take(len(PIECES))
    crossing, mortar, pairs, counts, wanted, asked = take(6)
    phi_sem, trace_sem, small_sem, ask_send, ask_recv = take(5)
    send_sem, recv_sem, cross_send, cross_recv, greeted_sem = take(5)

    owned, iface, modes = panels.shape
    npair = mortar.shape[0]
    row = lax.axis_index("row")
    col = lax.axis_index("col")
    mine = row * ncol + col
    near = [
        (lax.rem(row + nrow - 1, nrow), col),
        (lax.rem(row + 1, nrow), col),
        (row, lax.rem(col + ncol - 1, ncol)),
        (row, lax.rem(col + 1, ncol)),
    ]
    exists = [row > 0, row < nrow - 1, None, None]

    def where_near(d, action):
        if exists[d] is None:
            action()
        else:
            pl.when(exists[d])(action)

    odd = lax.rem(col, 2) == 1
    barrier = pltpu.get_barrier_semaphore()

    def greet(d):
        pl.semaphore_signal(barrier, inc=1, device_id=near[d], device_id_type=MESH)

    for d in ROW_STEPS:
        where_near(d, lambda: greet(d))

    @pl.when(jnp.logical_not(odd))
    def _():
        for d in COLUMN_STEPS:
            greet(d)

    def trace_copy(b, s):
        first, size = ROW_BLOCKS[b]
        return pltpu.make_async_copy(
            trace_hbm.at[s, pl.ds(first, size)], trace[b].at[s], trace_sem.at[b, s]
        )

    def phi_copy(b, s):
        first, size = COLUMN_BLOCKS[b]
        return pltpu.make_async_copy(
            phi_hbm.at[s, :, pl.ds(first, size)], phi[b].at[s], phi_sem.at[b, s]
        )

    pairs_copy = pltpu.make_async_copy(pairs_hbm, pairs, small_sem.at[0])
    counts_copy = pltpu.make_async_copy(counts_hbm, counts, small_sem.at[1])
    mortar_copy = pltpu.make_async_copy(mortar_hbm, mortar, small_sem.at[2])
    pairs_copy.start()
    counts_copy.start()

    loads = []
    for rows, columns in PIECES:
        loads += [(trace_copy, b) for b in rows if (trace_copy, b) not in loads]
        loads += [(phi_copy, b) for b in columns if (phi_copy, b) not in loads]
    for load, b in loads:
        @pl.loop(0, owned)
        def _(s):
            load(b, s).start()

    mortar_copy.start()
    pairs_copy.wait()
    counts_copy.wait()

    base = [(r * ncol + k) * owned for r, k in near]
    taken = [jnp.int32(0)] * 4
    first = [jnp.int32(0)] * 4
    second = [jnp.int32(0)] * 4
    for p in range(npair):
        j = pairs[1, p]
        place = jnp.clip(j - mine * owned, 0, owned - 1)
        for d in range(4):
            local = j - base[d]
            hit = (local >= 0) & (local < owned)
            first[d] = jnp.where(hit & (taken[d] == 0), local, first[d])
            second[d] = jnp.where(hit & (taken[d] == 1), local, second[d])
            slot = owned + CAP * d + jnp.minimum(taken[d], CAP - 1)
            place = jnp.where(hit, slot, place)
            taken[d] = taken[d] + hit.astype(jnp.int32)
        route[p] = place
    for d in range(4):
        wanted[d, 0] = first[d]
        wanted[d, 1] = second[d]

    greeted = exists[0].astype(jnp.int32) + exists[1].astype(jnp.int32)
    pl.semaphore_wait(barrier, greeted + jnp.where(odd, 2, 0))

    @pl.when(odd)
    def _():
        for d in COLUMN_STEPS:
            pl.semaphore_signal(
                greeted_sem, inc=1, device_id=near[d], device_id_type=MESH
            )

    asks = [
        pltpu.make_async_remote_copy(
            src_ref=wanted.at[d],
            dst_ref=asked.at[d ^ 1],
            send_sem=ask_send.at[d],
            recv_sem=ask_recv.at[d ^ 1],
            device_id=near[d],
            device_id_type=MESH,
        )
        for d in range(4)
    ]
    for d in ROW_STEPS:
        where_near(d, asks[d].start)

    def answer(d):
        where_near(d, asks[d ^ 1].wait_recv)

    def product(s, rows, columns):
        maps = jnp.concatenate([trace[b][s] for b in rows], axis=0)
        modes = jnp.concatenate([phi[b][s] for b in columns], axis=1)
        product = jnp.dot(maps, modes, preferred_element_type=jnp.float32)
        return product.astype(panels.dtype)

    waited = set()
    sends = []
    for n, (rows, columns) in enumerate(PIECES):
        fresh = [(trace_copy, b) for b in rows] + [(phi_copy, b) for b in columns]
        fresh = [item for item in fresh if item not in waited]
        waited.update(fresh)

        @pl.loop(0, owned)
        def _(s):
            for load, b in fresh:
                load(b, s).wait()

        for d in ROW_STEPS:
            if n == 0:
                answer(d)
            send = pltpu.make_async_remote_copy(
                src_ref=outgoing[n].at[d],
                dst_ref=arrived[n].at[d ^ 1],
                send_sem=send_sem.at[n, d],
                recv_sem=recv_sem.at[n, d ^ 1],
                device_id=near[d],
                device_id_type=MESH,
            )

            def project():
                for k in range(CAP):
                    outgoing[n][d, k] = product(asked[d, k], rows, columns)
                send.start()

            where_near(d, project)
            sends.append((d, send))
        if n == 0:
            @pl.when(jnp.logical_not(odd))
            def _():
                pl.semaphore_wait(greeted_sem, 2)

            for d in COLUMN_STEPS:
                asks[d].start()

    all_rows = tuple(range(len(ROW_BLOCKS)))
    all_columns = tuple(range(len(COLUMN_BLOCKS)))
    for d in COLUMN_STEPS:
        answer(d)
        for k in range(CAP):
            crossing[d - 2, k] = product(asked[d, k], all_rows, all_columns)
        send = pltpu.make_async_remote_copy(
            src_ref=crossing.at[d - 2],
            dst_ref=across.at[(d ^ 1) - 2],
            send_sem=cross_send.at[d - 2],
            recv_sem=cross_recv.at[(d ^ 1) - 2],
            device_id=near[d],
            device_id_type=MESH,
        )
        send.start()
        sends.append((d, send))

    @pl.loop(0, owned // GROUP)
    def _(g):
        for u in range(GROUP):
            panels[g * GROUP + u] = product(g * GROUP + u, all_rows, all_columns)

    mortar_copy.wait()
    row_ids = lax.broadcasted_iota(jnp.int32, (iface, iface), 0)
    column_ids = lax.broadcasted_iota(jnp.int32, (iface, iface), 1)

    @pl.loop(0, npair)
    def _(p):
        own = jnp.clip(pairs[0, p] - mine * owned, 0, owned - 1)
        count = counts[p]
        keep = (row_ids < count) & (column_ids < count)
        masked = jnp.where(keep, mortar[p].astype(jnp.float32), 0.0).astype(mortar.dtype)
        left[p] = lax.dot_general(
            panels[own],
            masked,
            (((0,), (0,)), ((), ())),
            preferred_element_type=jnp.float32,
        ).astype(left.dtype)

    for d in range(4):
        where_near(d, asks[d].wait_send)
    along_column = [item for item in sends if item[0] in COLUMN_STEPS]
    along_row = [item for item in sends if item[0] in ROW_STEPS]
    for d, send in along_column + along_row:
        where_near(d, send.wait_send)
    for d, send in along_column + along_row:
        where_near(d ^ 1, send.wait_recv)


def coupling_kernel(route, panels, left, across, *refs):
    arrived = refs[: len(PIECES)]
    coupling_hbm, coupling, out_sem = refs[len(PIECES) :]
    owned = panels.shape[0]
    copies = []
    for p in range(left.shape[0]):
        place = route[p]
        inside = jnp.minimum(place, owned - 1)
        slot = jnp.maximum(place - owned, 0)
        step = slot // CAP
        along_row = jnp.minimum(step, 1)
        along_column = jnp.maximum(step - 2, 0)
        k = slot % CAP
        columns = []
        for c in range(len(COLUMN_BLOCKS)):
            parts = [arrived[n][along_row, k] for n in range(len(PIECES)) if PIECES[n][1] == (c,)]
            columns.append(jnp.concatenate(parts, axis=0))
        partner = jnp.concatenate(columns, axis=1)
        partner = lax.select(step >= 2, across[along_column, k], partner)
        partner = lax.select(place < owned, panels[inside], partner)
        coupling[p] = jnp.dot(
            left[p], partner, preferred_element_type=jnp.float32
        ).astype(coupling.dtype)
        copy = pltpu.make_async_copy(coupling.at[p], coupling_hbm.at[p], out_sem.at[p])
        copy.start()
        copies.append(copy)
    for copy in copies:
        copy.wait()


def body(nrow, ncol, phi_modes, trace_maps, mortar, pair_list, iface_counts):
    owned, boundary, modes = phi_modes.shape
    npair, iface, _ = mortar.shape
    dtype = phi_modes.dtype
    hbm = pl.BlockSpec(memory_space=pltpu.HBM)
    smem = pl.BlockSpec(memory_space=pltpu.SMEM)
    vmem = pl.BlockSpec(memory_space=pltpu.VMEM)
    dma = pltpu.SemaphoreType.DMA
    count = len(PIECES)
    pieces = [
        pltpu.VMEM((2, CAP, extent(ROW_BLOCKS, r), extent(COLUMN_BLOCKS, c)), dtype)
        for r, c in PIECES
    ]
    across = pltpu.VMEM((2, CAP, iface, modes), dtype)
    panels, left, route, across_in, *arrived = pl.pallas_call(
        functools.partial(panels_kernel, nrow, ncol),
        out_shape=(
            pltpu.VMEM((owned, iface, modes), dtype),
            pltpu.VMEM((npair, modes, iface), dtype),
            pltpu.SMEM((npair,), jnp.int32),
            across,
            *pieces,
        ),
        in_specs=[hbm] * 5,
        out_specs=(vmem, vmem, smem, vmem, *[vmem] * count),
        scratch_shapes=[
            *[pltpu.VMEM((owned, boundary, size), dtype) for _, size in COLUMN_BLOCKS],
            *[pltpu.VMEM((owned, size, boundary), dtype) for _, size in ROW_BLOCKS],
            *pieces,
            across,
            pltpu.VMEM((npair, iface, iface), dtype),
            pltpu.SMEM((2, npair), jnp.int32),
            pltpu.SMEM((npair,), jnp.int32),
            pltpu.SMEM((4, 128), jnp.int32),
            pltpu.SMEM((4, 128), jnp.int32),
            dma((len(COLUMN_BLOCKS), owned)),
            dma((len(ROW_BLOCKS), owned)),
            dma((3,)),
            dma((4,)),
            dma((4,)),
            dma((count, 2)),
            dma((count, 2)),
            dma((2,)),
            dma((2,)),
            pltpu.SemaphoreType.REGULAR,
        ],
        compiler_params=pltpu.CompilerParams(
            collective_id=0, has_side_effects=True, vmem_limit_bytes=48 * 2**20
        ),
        name="panels",
    )(phi_modes, trace_maps, mortar, pair_list.T, iface_counts)
    return pl.pallas_call(
        coupling_kernel,
        out_shape=jax.ShapeDtypeStruct((npair, modes, modes), dtype),
        in_specs=[smem, vmem, vmem, vmem, *[vmem] * count],
        out_specs=hbm,
        scratch_shapes=[pltpu.VMEM((npair, modes, modes), dtype), dma((npair,))],
        compiler_params=pltpu.CompilerParams(vmem_limit_bytes=32 * 2**20),
        name="coupling",
    )(route, panels, left, across_in, *arrived)


def solution(mesh):
    return jax.shard_map(
        functools.partial(body, mesh.shape["row"], mesh.shape["col"]),
        mesh=mesh,
        in_specs=(
            P(("row", "col"), None, None),
            P(("row", "col"), None, None),
            P(("row", "col"), None, None),
            P(("row", "col"), None),
            P(("row", "col")),
        ),
        out_specs=P(("row", "col"), None, None),
        check_vma=False,
    )
```

```python
import functools

import jax
import jax.numpy as jnp
from jax import lax
from jax.experimental import pallas as pl
from jax.experimental.pallas import tpu as pltpu
from jax.sharding import PartitionSpec as P

MESH = pl.DeviceIdType.MESH
ROW_STEPS = (1, 0)
COLUMN_STEPS = (2, 3)
CAP = 2
ROW_BLOCKS = ((0, 128), (128, 128))
COLUMN_BLOCKS = ((0, 256), (256, 256))
PIECES = (((0,), (0,)), ((1,), (0,)), ((0, 1), (1,)))
PLANE = 4
PASSED = (((0,), 64, (0, 1)), ((0,), 64, (0, 1)), ((7, 0), 64, (0,)))
GROUP = 4


def extent(blocks, chosen):
    return sum(blocks[b][1] for b in chosen)


def panels_kernel(nrow, ncol, *refs):
    refs = list(refs)

    def take(count):
        taken = refs[:count]
        del refs[:count]
        return taken

    phi_hbm, trace_hbm, mortar_hbm, pairs_hbm, counts_hbm = take(5)
    panels, left, route, across = take(4)
    arrived = take(len(PIECES))
    phi = take(len(COLUMN_BLOCKS))
    trace = take(len(ROW_BLOCKS))
    outgoing = take(len(PIECES))
    crossing, mortar, pairs, counts, wanted, asked = take(6)
    phi_sem, trace_sem, small_sem, ask_send, ask_recv = take(5)
    send_sem, recv_sem, cross_send, cross_recv, greeted_sem = take(5)
    passing = take(len(PASSED))
    passing_recv, passing_send = take(2)

    owned, iface, modes = panels.shape
    npair = mortar.shape[0]
    row = lax.axis_index("row")
    col = lax.axis_index("col")
    mine = row * ncol + col
    near = [
        (lax.rem(row + nrow - 1, nrow), col),
        (lax.rem(row + 1, nrow), col),
        (row, lax.rem(col + ncol - 1, ncol)),
        (row, lax.rem(col + 1, ncol)),
    ]
    exists = [row > 0, row < nrow - 1, None, None]

    def where_near(d, action):
        if exists[d] is None:
            action()
        else:
            pl.when(exists[d])(action)

    ways = [
        (PLANE * x + PLANE - 1, *by, PLANE * (x + 1)) for x, (by, _, _) in enumerate(PASSED)
    ]

    odd = lax.rem(col, 2) == 1

    def is_at(x, place):
        if len(PASSED[x][2]) == 2:
            return row == place
        return (row == place) & (lax.rem(col, 2) == PASSED[x][2][0])

    barrier = pltpu.get_barrier_semaphore()

    def greet(d):
        pl.semaphore_signal(barrier, inc=1, device_id=near[d], device_id_type=MESH)

    for d in ROW_STEPS:
        where_near(d, lambda: greet(d))

    def greet_row(other):
        pl.semaphore_signal(
            barrier, inc=1, device_id=(jnp.int32(other), col), device_id_type=MESH
        )

    for x, way in enumerate(ways):
        for source, target in zip(way, way[1:]):
            pl.when(is_at(x, target))(lambda: greet_row(source))

    @pl.when(jnp.logical_not(odd))
    def _():
        for d in COLUMN_STEPS:
            greet(d)

    def trace_copy(b, s):
        first, size = ROW_BLOCKS[b]
        return pltpu.make_async_copy(
            trace_hbm.at[s, pl.ds(first, size)], trace[b].at[s], trace_sem.at[b, s]
        )

    def phi_copy(b, s):
        first, size = COLUMN_BLOCKS[b]
        return pltpu.make_async_copy(
            phi_hbm.at[s, :, pl.ds(first, size)], phi[b].at[s], phi_sem.at[b, s]
        )

    pairs_copy = pltpu.make_async_copy(pairs_hbm, pairs, small_sem.at[0])
    counts_copy = pltpu.make_async_copy(counts_hbm, counts, small_sem.at[1])
    mortar_copy = pltpu.make_async_copy(mortar_hbm, mortar, small_sem.at[2])
    pairs_copy.start()
    counts_copy.start()

    loads = []
    for rows, columns in PIECES:
        loads += [(trace_copy, b) for b in rows if (trace_copy, b) not in loads]
        loads += [(phi_copy, b) for b in columns if (phi_copy, b) not in loads]
    for load, b in loads:
        @pl.loop(0, owned)
        def _(s):
            load(b, s).start()

    mortar_copy.start()
    pairs_copy.wait()
    counts_copy.wait()

    base = [(r * ncol + k) * owned for r, k in near]
    taken = [jnp.int32(0)] * 4
    first = [jnp.int32(0)] * 4
    second = [jnp.int32(0)] * 4
    for p in range(npair):
        j = pairs[1, p]
        place = jnp.clip(j - mine * owned, 0, owned - 1)
        for d in range(4):
            local = j - base[d]
            hit = (local >= 0) & (local < owned)
            first[d] = jnp.where(hit & (taken[d] == 0), local, first[d])
            second[d] = jnp.where(hit & (taken[d] == 1), local, second[d])
            slot = owned + CAP * d + jnp.minimum(taken[d], CAP - 1)
            place = jnp.where(hit, slot, place)
            taken[d] = taken[d] + hit.astype(jnp.int32)
        route[p] = place
    for d in range(4):
        wanted[d, 0] = first[d]
        wanted[d, 1] = second[d]

    greeted = exists[0].astype(jnp.int32) + exists[1].astype(jnp.int32)
    for x, way in enumerate(ways):
        for source in way[:-1]:
            greeted = greeted + is_at(x, source).astype(jnp.int32)
    pl.semaphore_wait(barrier, greeted + jnp.where(odd, 2, 0))

    @pl.when(odd)
    def _():
        for d in COLUMN_STEPS:
            pl.semaphore_signal(
                greeted_sem, inc=1, device_id=near[d], device_id_type=MESH
            )

    asks = [
        pltpu.make_async_remote_copy(
            src_ref=wanted.at[d],
            dst_ref=asked.at[d ^ 1],
            send_sem=ask_send.at[d],
            recv_sem=ask_recv.at[d ^ 1],
            device_id=near[d],
            device_id_type=MESH,
        )
        for d in range(4)
    ]
    for d in ROW_STEPS:
        where_near(d, asks[d].start)

    def answer(d):
        where_near(d, asks[d ^ 1].wait_recv)

    def product(s, rows, columns):
        maps = jnp.concatenate([trace[b][s] for b in rows], axis=0)
        modes = jnp.concatenate([phi[b][s] for b in columns], axis=1)
        product = jnp.dot(maps, modes, preferred_element_type=jnp.float32)
        return product.astype(panels.dtype)

    def start_split(send):
        direct = row < nrow
        for x, way in enumerate(ways):
            size = PASSED[x][1]
            direct = direct & jnp.logical_not(is_at(x, way[0]))

            @pl.when(is_at(x, way[0]))
            def _():
                pltpu.make_async_remote_copy(
                    src_ref=outgoing[0].at[1, :, pl.ds(0, size)],
                    dst_ref=passing[x],
                    send_sem=send_sem.at[0, 1],
                    recv_sem=passing_recv.at[x],
                    device_id=(jnp.int32(way[1]), col),
                    device_id_type=MESH,
                ).start()
                rest = pl.ds(size, outgoing[0].shape[2] - size)
                pltpu.make_async_remote_copy(
                    src_ref=outgoing[0].at[1, :, rest],
                    dst_ref=arrived[0].at[0, :, rest],
                    send_sem=send_sem.at[0, 1],
                    recv_sem=recv_sem.at[0, 0],
                    device_id=near[1],
                    device_id_type=MESH,
                ).start()

        pl.when(direct)(send.start)

    def passed_on(x, hop):
        final = hop == len(ways[x]) - 2
        target = arrived[0].at[0, :, pl.ds(0, PASSED[x][1])]
        return pltpu.make_async_remote_copy(
            src_ref=passing[x],
            dst_ref=target if final else passing[x],
            send_sem=passing_send.at[x],
            recv_sem=recv_sem.at[0, 0] if final else passing_recv.at[x],
            device_id=(jnp.int32(ways[x][hop + 1]), col),
            device_id_type=MESH,
        )

    def pass_on(x, hop):
        way = ways[x]

        @pl.when(is_at(x, way[hop]))
        def _():
            pltpu.make_async_remote_copy(
                src_ref=passing[x],
                dst_ref=passing[x],
                send_sem=passing_send.at[x],
                recv_sem=passing_recv.at[x],
                device_id=(jnp.int32(way[hop + 1]), col),
                device_id_type=MESH,
            ).wait_recv()
            passed_on(x, hop).start()

    held = []
    waited = set()
    sends = []
    for n, (rows, columns) in enumerate(PIECES):
        fresh = [(trace_copy, b) for b in rows] + [(phi_copy, b) for b in columns]
        fresh = [item for item in fresh if item not in waited]
        waited.update(fresh)

        @pl.loop(0, owned)
        def _(s):
            for load, b in fresh:
                load(b, s).wait()

        for d in ROW_STEPS:
            if n == 0:
                answer(d)
            send = pltpu.make_async_remote_copy(
                src_ref=outgoing[n].at[d],
                dst_ref=arrived[n].at[d ^ 1],
                send_sem=send_sem.at[n, d],
                recv_sem=recv_sem.at[n, d ^ 1],
                device_id=near[d],
                device_id_type=MESH,
            )

            def project():
                for k in range(CAP):
                    outgoing[n][d, k] = product(asked[d, k], rows, columns)

            def start(n=n, d=d, send=send):
                if d == 1 and n == 0:
                    start_split(send)
                else:
                    send.start()

            where_near(d, project)
            if n == len(PIECES) - 1:
                held.append((d, start))
            else:
                where_near(d, start)
            sends.append((d, send))
        if n == 0:
            @pl.when(jnp.logical_not(odd))
            def _():
                pl.semaphore_wait(greeted_sem, 2)

            for d in COLUMN_STEPS:
                asks[d].start()

    pass_on(2, 1)
    for d, start in held:
        where_near(d, start)

    all_rows = tuple(range(len(ROW_BLOCKS)))
    all_columns = tuple(range(len(COLUMN_BLOCKS)))
    for d in COLUMN_STEPS:
        answer(d)
        for k in range(CAP):
            crossing[d - 2, k] = product(asked[d, k], all_rows, all_columns)
        send = pltpu.make_async_remote_copy(
            src_ref=crossing.at[d - 2],
            dst_ref=across.at[(d ^ 1) - 2],
            send_sem=cross_send.at[d - 2],
            recv_sem=cross_recv.at[(d ^ 1) - 2],
            device_id=near[d],
            device_id_type=MESH,
        )
        send.start()
        sends.append((d, send))

    @pl.loop(0, owned // GROUP)
    def _(g):
        for u in range(GROUP):
            panels[g * GROUP + u] = product(g * GROUP + u, all_rows, all_columns)

    pass_on(0, 1)
    pass_on(1, 1)
    pass_on(2, 2)
    mortar_copy.wait()
    row_ids = lax.broadcasted_iota(jnp.int32, (iface, iface), 0)
    column_ids = lax.broadcasted_iota(jnp.int32, (iface, iface), 1)

    @pl.loop(0, npair)
    def _(p):
        own = jnp.clip(pairs[0, p] - mine * owned, 0, owned - 1)
        count = counts[p]
        keep = (row_ids < count) & (column_ids < count)
        masked = jnp.where(keep, mortar[p].astype(jnp.float32), 0.0).astype(mortar.dtype)
        left[p] = lax.dot_general(
            panels[own],
            masked,
            (((0,), (0,)), ((), ())),
            preferred_element_type=jnp.float32,
        ).astype(left.dtype)

    for d in range(4):
        where_near(d, asks[d].wait_send)
    for x, way in enumerate(ways):
        for hop in range(1, len(way) - 1):
            pl.when(is_at(x, way[hop]))(passed_on(x, hop).wait_send)
    along_column = [item for item in sends if item[0] in COLUMN_STEPS]
    along_row = [item for item in sends if item[0] in ROW_STEPS]
    for d, send in along_column + along_row:
        where_near(d, send.wait_send)
    for d, send in along_column + along_row:
        where_near(d ^ 1, send.wait_recv)


def coupling_kernel(route, panels, left, across, *refs):
    arrived = refs[: len(PIECES)]
    coupling_hbm, coupling, out_sem = refs[len(PIECES) :]
    owned = panels.shape[0]
    copies = []
    for p in range(left.shape[0]):
        place = route[p]
        inside = jnp.minimum(place, owned - 1)
        slot = jnp.maximum(place - owned, 0)
        step = slot // CAP
        along_row = jnp.minimum(step, 1)
        along_column = jnp.maximum(step - 2, 0)
        k = slot % CAP
        columns = []
        for c in range(len(COLUMN_BLOCKS)):
            parts = [arrived[n][along_row, k] for n in range(len(PIECES)) if PIECES[n][1] == (c,)]
            columns.append(jnp.concatenate(parts, axis=0))
        partner = jnp.concatenate(columns, axis=1)
        partner = lax.select(step >= 2, across[along_column, k], partner)
        partner = lax.select(place < owned, panels[inside], partner)
        coupling[p] = jnp.dot(
            left[p], partner, preferred_element_type=jnp.float32
        ).astype(coupling.dtype)
        copy = pltpu.make_async_copy(coupling.at[p], coupling_hbm.at[p], out_sem.at[p])
        copy.start()
        copies.append(copy)
    for copy in copies:
        copy.wait()


def body(nrow, ncol, phi_modes, trace_maps, mortar, pair_list, iface_counts):
    owned, boundary, modes = phi_modes.shape
    npair, iface, _ = mortar.shape
    dtype = phi_modes.dtype
    hbm = pl.BlockSpec(memory_space=pltpu.HBM)
    smem = pl.BlockSpec(memory_space=pltpu.SMEM)
    vmem = pl.BlockSpec(memory_space=pltpu.VMEM)
    dma = pltpu.SemaphoreType.DMA
    count = len(PIECES)
    pieces = [
        pltpu.VMEM((2, CAP, extent(ROW_BLOCKS, r), extent(COLUMN_BLOCKS, c)), dtype)
        for r, c in PIECES
    ]
    across = pltpu.VMEM((2, CAP, iface, modes), dtype)
    panels, left, route, across_in, *arrived = pl.pallas_call(
        functools.partial(panels_kernel, nrow, ncol),
        out_shape=(
            pltpu.VMEM((owned, iface, modes), dtype),
            pltpu.VMEM((npair, modes, iface), dtype),
            pltpu.SMEM((npair,), jnp.int32),
            across,
            *pieces,
        ),
        in_specs=[hbm] * 5,
        out_specs=(vmem, vmem, smem, vmem, *[vmem] * count),
        scratch_shapes=[
            *[pltpu.VMEM((owned, boundary, size), dtype) for _, size in COLUMN_BLOCKS],
            *[pltpu.VMEM((owned, size, boundary), dtype) for _, size in ROW_BLOCKS],
            *pieces,
            across,
            pltpu.VMEM((npair, iface, iface), dtype),
            pltpu.SMEM((2, npair), jnp.int32),
            pltpu.SMEM((npair,), jnp.int32),
            pltpu.SMEM((4, 128), jnp.int32),
            pltpu.SMEM((4, 128), jnp.int32),
            dma((len(COLUMN_BLOCKS), owned)),
            dma((len(ROW_BLOCKS), owned)),
            dma((3,)),
            dma((4,)),
            dma((4,)),
            dma((count, 2)),
            dma((count, 2)),
            dma((2,)),
            dma((2,)),
            pltpu.SemaphoreType.REGULAR,
            *[pltpu.VMEM((CAP, size, pieces[0].shape[3]), dtype) for _, size, _ in PASSED],
            dma((len(PASSED),)),
            dma((len(PASSED),)),
        ],
        compiler_params=pltpu.CompilerParams(
            collective_id=0, has_side_effects=True, vmem_limit_bytes=48 * 2**20
        ),
        name="panels",
    )(phi_modes, trace_maps, mortar, pair_list.T, iface_counts)
    return pl.pallas_call(
        coupling_kernel,
        out_shape=jax.ShapeDtypeStruct((npair, modes, modes), dtype),
        in_specs=[smem, vmem, vmem, vmem, *[vmem] * count],
        out_specs=hbm,
        scratch_shapes=[pltpu.VMEM((npair, modes, modes), dtype), dma((npair,))],
        compiler_params=pltpu.CompilerParams(vmem_limit_bytes=32 * 2**20),
        name="coupling",
    )(route, panels, left, across_in, *arrived)


def solution(mesh):
    return jax.shard_map(
        functools.partial(body, mesh.shape["row"], mesh.shape["col"]),
        mesh=mesh,
        in_specs=(
            P(("row", "col"), None, None),
            P(("row", "col"), None, None),
            P(("row", "col"), None, None),
            P(("row", "col"), None),
            P(("row", "col")),
        ),
        out_specs=P(("row", "col"), None, None),
        check_vma=False,
    )
```

```python
import functools

import jax
import jax.numpy as jnp
from jax import lax
from jax.experimental import pallas as pl
from jax.experimental.pallas import tpu as pltpu
from jax.sharding import PartitionSpec as P

MESH = pl.DeviceIdType.MESH
ROW_STEPS = (1, 0)
COLUMN_STEPS = (2, 3)
CAP = 2
ROW_BLOCKS = ((0, 128), (128, 128))
COLUMN_BLOCKS = ((0, 256), (256, 256))
PIECES = (((0,), (0,)), ((1,), (0,)), ((0, 1), (1,)))
PLANE = 4
PASSED = (((0,), 64, (0, 1)), ((0,), 64, (0, 1)), ((7, 0), 64, (0,)))
FIRST_PARTS = 2
GROUP = 4


def extent(blocks, chosen):
    return sum(blocks[b][1] for b in chosen)


def panels_kernel(nrow, ncol, *refs):
    refs = list(refs)

    def take(count):
        taken = refs[:count]
        del refs[:count]
        return taken

    phi_hbm, trace_hbm, mortar_hbm, pairs_hbm, counts_hbm = take(5)
    table, left, route = take(3)
    phi = take(len(COLUMN_BLOCKS))
    trace = take(len(ROW_BLOCKS))
    outgoing = take(len(PIECES))
    crossing, panels, mortar, pairs, counts, wanted, asked = take(7)
    phi_sem, trace_sem, small_sem, ask_send, ask_recv = take(5)
    send_sem, recv_sem, cross_send, cross_recv, greeted_sem = take(5)
    passing = take(len(PASSED))
    passing_recv, passing_send = take(2)

    owned, iface, modes = panels.shape
    npair = mortar.shape[0]
    row = lax.axis_index("row")
    col = lax.axis_index("col")
    mine = row * ncol + col
    near = [
        (lax.rem(row + nrow - 1, nrow), col),
        (lax.rem(row + 1, nrow), col),
        (row, lax.rem(col + ncol - 1, ncol)),
        (row, lax.rem(col + 1, ncol)),
    ]
    exists = [row > 0, row < nrow - 1, None, None]

    def where_near(d, action):
        if exists[d] is None:
            action()
        else:
            pl.when(exists[d])(action)

    ways = [
        (PLANE * x + PLANE - 1, *by, PLANE * (x + 1)) for x, (by, _, _) in enumerate(PASSED)
    ]

    odd = lax.rem(col, 2) == 1

    def is_at(x, place):
        if len(PASSED[x][2]) == 2:
            return row == place
        return (row == place) & (lax.rem(col, 2) == PASSED[x][2][0])

    barrier = pltpu.get_barrier_semaphore()

    def greet(d):
        pl.semaphore_signal(barrier, inc=1, device_id=near[d], device_id_type=MESH)

    for d in ROW_STEPS:
        where_near(d, lambda: greet(d))

    def greet_row(other):
        pl.semaphore_signal(
            barrier, inc=1, device_id=(jnp.int32(other), col), device_id_type=MESH
        )

    for x, way in enumerate(ways):
        for source, target in zip(way, way[1:]):
            pl.when(is_at(x, target))(lambda: greet_row(source))

    @pl.when(jnp.logical_not(odd))
    def _():
        for d in COLUMN_STEPS:
            greet(d)

    def trace_copy(b, s):
        first, size = ROW_BLOCKS[b]
        return pltpu.make_async_copy(
            trace_hbm.at[s, pl.ds(first, size)], trace[b].at[s], trace_sem.at[b, s]
        )

    def phi_copy(b, s):
        first, size = COLUMN_BLOCKS[b]
        return pltpu.make_async_copy(
            phi_hbm.at[s, :, pl.ds(first, size)], phi[b].at[s], phi_sem.at[b, s]
        )

    pairs_copy = pltpu.make_async_copy(pairs_hbm, pairs, small_sem.at[0])
    counts_copy = pltpu.make_async_copy(counts_hbm, counts, small_sem.at[1])
    mortar_copy = pltpu.make_async_copy(mortar_hbm, mortar, small_sem.at[2])
    pairs_copy.start()
    counts_copy.start()

    loads = []
    for rows, columns in PIECES:
        loads += [(trace_copy, b) for b in rows if (trace_copy, b) not in loads]
        loads += [(phi_copy, b) for b in columns if (phi_copy, b) not in loads]
    for load, b in loads:
        @pl.loop(0, owned)
        def _(s):
            load(b, s).start()

    mortar_copy.start()
    pairs_copy.wait()
    counts_copy.wait()

    base = [(r * ncol + k) * owned for r, k in near]
    taken = [jnp.int32(0)] * 4
    first = [jnp.int32(0)] * 4
    second = [jnp.int32(0)] * 4
    for p in range(npair):
        j = pairs[1, p]
        place = jnp.clip(j - mine * owned, 0, owned - 1)
        for d in range(4):
            local = j - base[d]
            hit = (local >= 0) & (local < owned)
            first[d] = jnp.where(hit & (taken[d] == 0), local, first[d])
            second[d] = jnp.where(hit & (taken[d] == 1), local, second[d])
            slot = owned + CAP * d + jnp.minimum(taken[d], CAP - 1)
            place = jnp.where(hit, slot, place)
            taken[d] = taken[d] + hit.astype(jnp.int32)
        route[p] = place
    for d in range(4):
        wanted[d, 0] = first[d]
        wanted[d, 1] = second[d]

    greeted = exists[0].astype(jnp.int32) + exists[1].astype(jnp.int32)
    for x, way in enumerate(ways):
        for source in way[:-1]:
            greeted = greeted + is_at(x, source).astype(jnp.int32)
    pl.semaphore_wait(barrier, greeted + jnp.where(odd, 2, 0))

    @pl.when(odd)
    def _():
        for d in COLUMN_STEPS:
            pl.semaphore_signal(
                greeted_sem, inc=1, device_id=near[d], device_id_type=MESH
            )

    asks = [
        pltpu.make_async_remote_copy(
            src_ref=wanted.at[d],
            dst_ref=asked.at[d ^ 1],
            send_sem=ask_send.at[d],
            recv_sem=ask_recv.at[d ^ 1],
            device_id=near[d],
            device_id_type=MESH,
        )
        for d in range(4)
    ]
    for d in ROW_STEPS:
        where_near(d, asks[d].start)

    def answer(d):
        where_near(d, asks[d ^ 1].wait_recv)

    def arriving(d, rows, columns):
        return table.at[pl.ds(owned + CAP * d, CAP), pl.ds(*rows), pl.ds(*columns)]

    def piece_arriving(n, d, first=0, size=None):
        rows, columns = PIECES[n]
        size = extent(ROW_BLOCKS, rows) if size is None else size
        return arriving(
            d,
            (ROW_BLOCKS[rows[0]][0] + first, size),
            (COLUMN_BLOCKS[columns[0]][0], extent(COLUMN_BLOCKS, columns)),
        )

    def product(s, rows, columns):
        maps = jnp.concatenate([trace[b][s] for b in rows], axis=0)
        modes = jnp.concatenate([phi[b][s] for b in columns], axis=1)
        product = jnp.dot(maps, modes, preferred_element_type=jnp.float32)
        return product.astype(panels.dtype)

    def start_split(send):
        direct = row < nrow
        for x, way in enumerate(ways):
            size = PASSED[x][1]
            direct = direct & jnp.logical_not(is_at(x, way[0]))

            @pl.when(is_at(x, way[0]))
            def _():
                pltpu.make_async_remote_copy(
                    src_ref=outgoing[0].at[1, :, pl.ds(0, size)],
                    dst_ref=passing[x],
                    send_sem=send_sem.at[0, 1],
                    recv_sem=passing_recv.at[x],
                    device_id=(jnp.int32(way[1]), col),
                    device_id_type=MESH,
                ).start()
                kept = outgoing[0].shape[2] - size
                pltpu.make_async_remote_copy(
                    src_ref=outgoing[0].at[1, :, pl.ds(size, kept)],
                    dst_ref=piece_arriving(0, 0, size, kept),
                    send_sem=send_sem.at[0, 1],
                    recv_sem=recv_sem.at[0, 0],
                    device_id=near[1],
                    device_id_type=MESH,
                ).start()

        pl.when(direct)(send.start)

    def passed_on(x, hop):
        final = hop == len(ways[x]) - 2
        target = piece_arriving(0, 0, 0, PASSED[x][1])
        return pltpu.make_async_remote_copy(
            src_ref=passing[x],
            dst_ref=target if final else passing[x],
            send_sem=passing_send.at[x],
            recv_sem=recv_sem.at[0, 0] if final else passing_recv.at[x],
            device_id=(jnp.int32(ways[x][hop + 1]), col),
            device_id_type=MESH,
        )

    def pass_on(x, hop):
        way = ways[x]

        @pl.when(is_at(x, way[hop]))
        def _():
            pltpu.make_async_remote_copy(
                src_ref=passing[x],
                dst_ref=passing[x],
                send_sem=passing_send.at[x],
                recv_sem=passing_recv.at[x],
                device_id=(jnp.int32(way[hop + 1]), col),
                device_id_type=MESH,
            ).wait_recv()
            passed_on(x, hop).start()

    def piece_send(n, d):
        return pltpu.make_async_remote_copy(
            src_ref=outgoing[n].at[d],
            dst_ref=piece_arriving(n, d ^ 1),
            send_sem=send_sem.at[n, d],
            recv_sem=recv_sem.at[n, d ^ 1],
            device_id=near[d],
            device_id_type=MESH,
        )

    def project(n, d):
        for k in range(CAP):
            outgoing[n][d, k] = product(asked[d, k], *PIECES[n])

    def start(n, d):
        if d == 1 and n == 0:
            start_split(piece_send(n, d))
        else:
            piece_send(n, d).start()

    def serve(n, order):
        for d in order:
            if n == 0:
                answer(d)
            where_near(d, lambda: project(n, d))
            where_near(d, lambda: start(n, d))

    waited = set()
    sends = []
    for n, (rows, columns) in enumerate(PIECES):
        fresh = [(trace_copy, b) for b in rows] + [(phi_copy, b) for b in columns]
        fresh = [item for item in fresh if item not in waited]
        waited.update(fresh)

        @pl.loop(0, owned)
        def _(s):
            for load, b in fresh:
                load(b, s).wait()

        if n < len(PIECES) - 1:
            serve(n, ROW_STEPS)
        else:
            midway = is_at(2, ways[2][1])

            @pl.when(jnp.logical_not(midway))
            def _():
                serve(n, ROW_STEPS)

            @pl.when(midway)
            def _():
                for d in ROW_STEPS:
                    where_near(d, lambda: project(n, d))
                pass_on(2, 1)
                for d in ROW_STEPS:
                    where_near(d, lambda: start(n, d))

        sends += [(d, piece_send(n, d)) for d in ROW_STEPS]
        if n == 0:
            @pl.when(jnp.logical_not(odd))
            def _():
                pl.semaphore_wait(greeted_sem, 2)

            for d in COLUMN_STEPS:
                asks[d].start()

    all_rows = tuple(range(len(ROW_BLOCKS)))
    all_columns = tuple(range(len(COLUMN_BLOCKS)))
    for d in COLUMN_STEPS:
        answer(d)
        for k in range(CAP):
            crossing[d - 2, k] = product(asked[d, k], all_rows, all_columns)
        send = pltpu.make_async_remote_copy(
            src_ref=crossing.at[d - 2],
            dst_ref=arriving(d ^ 1, (0, iface), (0, modes)),
            send_sem=cross_send.at[d - 2],
            recv_sem=cross_recv.at[(d ^ 1) - 2],
            device_id=near[d],
            device_id_type=MESH,
        )
        send.start()
        sends.append((d, send))

    @pl.loop(0, owned // GROUP)
    def _(g):
        for u in range(GROUP):
            panel = product(g * GROUP + u, all_rows, all_columns)
            panels[g * GROUP + u] = panel
            table[g * GROUP + u] = panel

    pass_on(0, 1)
    pass_on(1, 1)
    pass_on(2, 2)
    mortar_copy.wait()
    row_ids = lax.broadcasted_iota(jnp.int32, (iface, iface), 0)
    column_ids = lax.broadcasted_iota(jnp.int32, (iface, iface), 1)

    @pl.loop(0, npair)
    def _(p):
        own = jnp.clip(pairs[0, p] - mine * owned, 0, owned - 1)
        count = counts[p]
        keep = (row_ids < count) & (column_ids < count)
        masked = jnp.where(keep, mortar[p].astype(jnp.float32), 0.0).astype(mortar.dtype)
        left[p] = lax.dot_general(
            panels[own],
            masked,
            (((0,), (0,)), ((), ())),
            preferred_element_type=jnp.float32,
        ).astype(left.dtype)

    for d in range(4):
        where_near(d, asks[d].wait_send)
    for x, way in enumerate(ways):
        for hop in range(1, len(way) - 1):
            pl.when(is_at(x, way[hop]))(passed_on(x, hop).wait_send)
    along_column = [item for item in sends if item[0] in COLUMN_STEPS]
    along_row = [item for item in sends if item[0] in ROW_STEPS]
    for d, send in along_column + along_row:
        where_near(d, send.wait_send)
    for d, send in along_column + along_row:
        where_near(d ^ 1, send.wait_recv)


def coupling_kernel(route, table, left, coupling_hbm, coupling, out_sem):
    npair, modes, _ = left.shape
    copies = []
    for p in range(npair):
        partner = table[route[p]]
        parts = FIRST_PARTS if p == 0 else 1
        rows = modes // parts
        for part in range(parts):
            block = (p, pl.ds(part * rows, rows))
            coupling[block] = jnp.dot(
                left[block], partner, preferred_element_type=jnp.float32
            ).astype(coupling.dtype)
            copy = pltpu.make_async_copy(
                coupling.at[block], coupling_hbm.at[block], out_sem.at[len(copies)]
            )
            copy.start()
            copies.append(copy)
    for copy in copies:
        copy.wait()


def body(nrow, ncol, phi_modes, trace_maps, mortar, pair_list, iface_counts):
    owned, boundary, modes = phi_modes.shape
    npair, iface, _ = mortar.shape
    dtype = phi_modes.dtype
    hbm = pl.BlockSpec(memory_space=pltpu.HBM)
    smem = pl.BlockSpec(memory_space=pltpu.SMEM)
    vmem = pl.BlockSpec(memory_space=pltpu.VMEM)
    dma = pltpu.SemaphoreType.DMA
    count = len(PIECES)
    pieces = [
        pltpu.VMEM((2, CAP, extent(ROW_BLOCKS, r), extent(COLUMN_BLOCKS, c)), dtype)
        for r, c in PIECES
    ]
    table, left, route = pl.pallas_call(
        functools.partial(panels_kernel, nrow, ncol),
        out_shape=(
            pltpu.VMEM((owned + 4 * CAP, iface, modes), dtype),
            pltpu.VMEM((npair, modes, iface), dtype),
            pltpu.SMEM((npair,), jnp.int32),
        ),
        in_specs=[hbm] * 5,
        out_specs=(vmem, vmem, smem),
        scratch_shapes=[
            *[pltpu.VMEM((owned, boundary, size), dtype) for _, size in COLUMN_BLOCKS],
            *[pltpu.VMEM((owned, size, boundary), dtype) for _, size in ROW_BLOCKS],
            *pieces,
            pltpu.VMEM((2, CAP, iface, modes), dtype),
            pltpu.VMEM((owned, iface, modes), dtype),
            pltpu.VMEM((npair, iface, iface), dtype),
            pltpu.SMEM((2, npair), jnp.int32),
            pltpu.SMEM((npair,), jnp.int32),
            pltpu.SMEM((4, 128), jnp.int32),
            pltpu.SMEM((4, 128), jnp.int32),
            dma((len(COLUMN_BLOCKS), owned)),
            dma((len(ROW_BLOCKS), owned)),
            dma((3,)),
            dma((4,)),
            dma((4,)),
            dma((count, 2)),
            dma((count, 2)),
            dma((2,)),
            dma((2,)),
            pltpu.SemaphoreType.REGULAR,
            *[pltpu.VMEM((CAP, size, pieces[0].shape[3]), dtype) for _, size, _ in PASSED],
            dma((len(PASSED),)),
            dma((len(PASSED),)),
        ],
        compiler_params=pltpu.CompilerParams(
            collective_id=0, has_side_effects=True, vmem_limit_bytes=48 * 2**20
        ),
        name="panels",
    )(phi_modes, trace_maps, mortar, pair_list.T, iface_counts)
    return pl.pallas_call(
        coupling_kernel,
        out_shape=jax.ShapeDtypeStruct((npair, modes, modes), dtype),
        in_specs=[smem, vmem, vmem],
        out_specs=hbm,
        scratch_shapes=[pltpu.VMEM((npair, modes, modes), dtype), dma((npair + FIRST_PARTS - 1,))],
        compiler_params=pltpu.CompilerParams(vmem_limit_bytes=32 * 2**20),
        name="coupling",
    )(route, table, left)


def solution(mesh):
    return jax.shard_map(
        functools.partial(body, mesh.shape["row"], mesh.shape["col"]),
        mesh=mesh,
        in_specs=(
            P(("row", "col"), None, None),
            P(("row", "col"), None, None),
            P(("row", "col"), None, None),
            P(("row", "col"), None),
            P(("row", "col")),
        ),
        out_specs=P(("row", "col"), None, None),
        check_vma=False,
    )
```

```python
import functools

import jax
import jax.numpy as jnp
from jax import lax
from jax.experimental import pallas as pl
from jax.experimental.pallas import tpu as pltpu
from jax.sharding import PartitionSpec as P

MESH = pl.DeviceIdType.MESH
ROW_STEPS = (1, 0)
COLUMN_STEPS = (2, 3)
CAP = 2
ROW_BLOCKS = ((0, 128), (128, 128))
COLUMN_BLOCKS = ((0, 256), (256, 256))
PIECES = (((0,), (0,)), ((1,), (0,)), ((0, 1), (1,)))
PLANE = 4
PASSED = (((0,), 96, (0, 1)), ((0,), 96, (0, 1)), ((7, 0), 64, (0,)))
FIRST_PARTS = 2
GROUP = 4


def extent(blocks, chosen):
    return sum(blocks[b][1] for b in chosen)


def panels_kernel(nrow, ncol, *refs):
    refs = list(refs)

    def take(count):
        taken = refs[:count]
        del refs[:count]
        return taken

    phi_hbm, trace_hbm, mortar_hbm, pairs_hbm, counts_hbm = take(5)
    table, left, route = take(3)
    phi = take(len(COLUMN_BLOCKS))
    trace = take(len(ROW_BLOCKS))
    outgoing = take(len(PIECES))
    crossing, panels, mortar, pairs, counts, wanted, asked = take(7)
    phi_sem, trace_sem, small_sem, ask_send, ask_recv = take(5)
    send_sem, recv_sem, cross_send, cross_recv, greeted_sem = take(5)
    passing = take(len(PASSED))
    passing_recv, passing_send = take(2)

    owned, iface, modes = panels.shape
    npair = mortar.shape[0]
    row = lax.axis_index("row")
    col = lax.axis_index("col")
    mine = row * ncol + col
    near = [
        (lax.rem(row + nrow - 1, nrow), col),
        (lax.rem(row + 1, nrow), col),
        (row, lax.rem(col + ncol - 1, ncol)),
        (row, lax.rem(col + 1, ncol)),
    ]
    exists = [row > 0, row < nrow - 1, None, None]

    def where_near(d, action):
        if exists[d] is None:
            action()
        else:
            pl.when(exists[d])(action)

    ways = [
        (PLANE * x + PLANE - 1, *by, PLANE * (x + 1)) for x, (by, _, _) in enumerate(PASSED)
    ]

    odd = lax.rem(col, 2) == 1

    def is_at(x, place):
        if len(PASSED[x][2]) == 2:
            return row == place
        return (row == place) & (lax.rem(col, 2) == PASSED[x][2][0])

    barrier = pltpu.get_barrier_semaphore()

    def greet(d):
        pl.semaphore_signal(barrier, inc=1, device_id=near[d], device_id_type=MESH)

    for d in ROW_STEPS:
        where_near(d, lambda: greet(d))

    def greet_row(other):
        pl.semaphore_signal(
            barrier, inc=1, device_id=(jnp.int32(other), col), device_id_type=MESH
        )

    for x, way in enumerate(ways):
        for source, target in zip(way, way[1:]):
            pl.when(is_at(x, target))(lambda: greet_row(source))

    @pl.when(jnp.logical_not(odd))
    def _():
        for d in COLUMN_STEPS:
            greet(d)

    def trace_copy(b, s):
        first, size = ROW_BLOCKS[b]
        return pltpu.make_async_copy(
            trace_hbm.at[s, pl.ds(first, size)], trace[b].at[s], trace_sem.at[b, s]
        )

    def phi_copy(b, s):
        first, size = COLUMN_BLOCKS[b]
        return pltpu.make_async_copy(
            phi_hbm.at[s, :, pl.ds(first, size)], phi[b].at[s], phi_sem.at[b, s]
        )

    pairs_copy = pltpu.make_async_copy(pairs_hbm, pairs, small_sem.at[0])
    counts_copy = pltpu.make_async_copy(counts_hbm, counts, small_sem.at[1])
    mortar_copy = pltpu.make_async_copy(mortar_hbm, mortar, small_sem.at[2])
    pairs_copy.start()
    counts_copy.start()

    loads = []
    for rows, columns in PIECES:
        loads += [(trace_copy, b) for b in rows if (trace_copy, b) not in loads]
        loads += [(phi_copy, b) for b in columns if (phi_copy, b) not in loads]
    for load, b in loads:
        @pl.loop(0, owned)
        def _(s):
            load(b, s).start()

    mortar_copy.start()
    pairs_copy.wait()
    counts_copy.wait()

    base = [(r * ncol + k) * owned for r, k in near]
    taken = [jnp.int32(0)] * 4
    first = [jnp.int32(0)] * 4
    second = [jnp.int32(0)] * 4
    for p in range(npair):
        j = pairs[1, p]
        place = jnp.clip(j - mine * owned, 0, owned - 1)
        for d in range(4):
            local = j - base[d]
            hit = (local >= 0) & (local < owned)
            first[d] = jnp.where(hit & (taken[d] == 0), local, first[d])
            second[d] = jnp.where(hit & (taken[d] == 1), local, second[d])
            slot = owned + CAP * d + jnp.minimum(taken[d], CAP - 1)
            place = jnp.where(hit, slot, place)
            taken[d] = taken[d] + hit.astype(jnp.int32)
        route[p] = place
    for d in range(4):
        wanted[d, 0] = first[d]
        wanted[d, 1] = second[d]

    greeted = exists[0].astype(jnp.int32) + exists[1].astype(jnp.int32)
    for x, way in enumerate(ways):
        for source in way[:-1]:
            greeted = greeted + is_at(x, source).astype(jnp.int32)
    pl.semaphore_wait(barrier, greeted + jnp.where(odd, 2, 0))

    @pl.when(odd)
    def _():
        for d in COLUMN_STEPS:
            pl.semaphore_signal(
                greeted_sem, inc=1, device_id=near[d], device_id_type=MESH
            )

    asks = [
        pltpu.make_async_remote_copy(
            src_ref=wanted.at[d],
            dst_ref=asked.at[d ^ 1],
            send_sem=ask_send.at[d],
            recv_sem=ask_recv.at[d ^ 1],
            device_id=near[d],
            device_id_type=MESH,
        )
        for d in range(4)
    ]
    for d in ROW_STEPS:
        where_near(d, asks[d].start)

    def answer(d):
        where_near(d, asks[d ^ 1].wait_recv)

    def arriving(d, rows, columns):
        return table.at[pl.ds(owned + CAP * d, CAP), pl.ds(*rows), pl.ds(*columns)]

    def piece_arriving(n, d, first=0, size=None):
        rows, columns = PIECES[n]
        size = extent(ROW_BLOCKS, rows) if size is None else size
        return arriving(
            d,
            (ROW_BLOCKS[rows[0]][0] + first, size),
            (COLUMN_BLOCKS[columns[0]][0], extent(COLUMN_BLOCKS, columns)),
        )

    def product(s, rows, columns):
        maps = jnp.concatenate([trace[b][s] for b in rows], axis=0)
        modes = jnp.concatenate([phi[b][s] for b in columns], axis=1)
        product = jnp.dot(maps, modes, preferred_element_type=jnp.float32)
        return product.astype(panels.dtype)

    def start_split(send):
        direct = row < nrow
        for x, way in enumerate(ways):
            size = PASSED[x][1]
            direct = direct & jnp.logical_not(is_at(x, way[0]))

            @pl.when(is_at(x, way[0]))
            def _():
                pltpu.make_async_remote_copy(
                    src_ref=outgoing[0].at[1, :, pl.ds(0, size)],
                    dst_ref=passing[x],
                    send_sem=send_sem.at[0, 1],
                    recv_sem=passing_recv.at[x],
                    device_id=(jnp.int32(way[1]), col),
                    device_id_type=MESH,
                ).start()
                kept = outgoing[0].shape[2] - size
                pltpu.make_async_remote_copy(
                    src_ref=outgoing[0].at[1, :, pl.ds(size, kept)],
                    dst_ref=piece_arriving(0, 0, size, kept),
                    send_sem=send_sem.at[0, 1],
                    recv_sem=recv_sem.at[0, 0],
                    device_id=near[1],
                    device_id_type=MESH,
                ).start()

        pl.when(direct)(send.start)

    def passed_on(x, hop):
        final = hop == len(ways[x]) - 2
        target = piece_arriving(0, 0, 0, PASSED[x][1])
        return pltpu.make_async_remote_copy(
            src_ref=passing[x],
            dst_ref=target if final else passing[x],
            send_sem=passing_send.at[x],
            recv_sem=recv_sem.at[0, 0] if final else passing_recv.at[x],
            device_id=(jnp.int32(ways[x][hop + 1]), col),
            device_id_type=MESH,
        )

    def pass_on(x, hop):
        way = ways[x]

        @pl.when(is_at(x, way[hop]))
        def _():
            pltpu.make_async_remote_copy(
                src_ref=passing[x],
                dst_ref=passing[x],
                send_sem=passing_send.at[x],
                recv_sem=passing_recv.at[x],
                device_id=(jnp.int32(way[hop + 1]), col),
                device_id_type=MESH,
            ).wait_recv()
            passed_on(x, hop).start()

    def piece_send(n, d):
        return pltpu.make_async_remote_copy(
            src_ref=outgoing[n].at[d],
            dst_ref=piece_arriving(n, d ^ 1),
            send_sem=send_sem.at[n, d],
            recv_sem=recv_sem.at[n, d ^ 1],
            device_id=near[d],
            device_id_type=MESH,
        )

    def project(n, d):
        for k in range(CAP):
            outgoing[n][d, k] = product(asked[d, k], *PIECES[n])

    def start(n, d):
        if d == 1 and n == 0:
            start_split(piece_send(n, d))
        else:
            piece_send(n, d).start()

    def serve(n, order):
        for d in order:
            if n == 0:
                answer(d)
            where_near(d, lambda: project(n, d))
            where_near(d, lambda: start(n, d))

    waited = set()
    sends = []
    for n, (rows, columns) in enumerate(PIECES):
        fresh = [(trace_copy, b) for b in rows] + [(phi_copy, b) for b in columns]
        fresh = [item for item in fresh if item not in waited]
        waited.update(fresh)

        @pl.loop(0, owned)
        def _(s):
            for load, b in fresh:
                load(b, s).wait()

        if n < len(PIECES) - 1:
            serve(n, ROW_STEPS)
        else:
            midway = is_at(2, ways[2][1])

            @pl.when(jnp.logical_not(midway))
            def _():
                serve(n, ROW_STEPS)

            @pl.when(midway)
            def _():
                for d in ROW_STEPS:
                    where_near(d, lambda: project(n, d))
                pass_on(2, 1)
                for d in ROW_STEPS:
                    where_near(d, lambda: start(n, d))

        sends += [(d, piece_send(n, d)) for d in ROW_STEPS]
        if n == 0:
            @pl.when(jnp.logical_not(odd))
            def _():
                pl.semaphore_wait(greeted_sem, 2)

            for d in COLUMN_STEPS:
                asks[d].start()

    all_rows = tuple(range(len(ROW_BLOCKS)))
    all_columns = tuple(range(len(COLUMN_BLOCKS)))
    for d in COLUMN_STEPS:
        answer(d)
        for k in range(CAP):
            crossing[d - 2, k] = product(asked[d, k], all_rows, all_columns)
        send = pltpu.make_async_remote_copy(
            src_ref=crossing.at[d - 2],
            dst_ref=arriving(d ^ 1, (0, iface), (0, modes)),
            send_sem=cross_send.at[d - 2],
            recv_sem=cross_recv.at[(d ^ 1) - 2],
            device_id=near[d],
            device_id_type=MESH,
        )
        send.start()
        sends.append((d, send))

    @pl.loop(0, owned // GROUP)
    def _(g):
        for u in range(GROUP):
            panel = product(g * GROUP + u, all_rows, all_columns)
            panels[g * GROUP + u] = panel
            table[g * GROUP + u] = panel

    pass_on(0, 1)
    pass_on(1, 1)
    pass_on(2, 2)
    mortar_copy.wait()
    row_ids = lax.broadcasted_iota(jnp.int32, (iface, iface), 0)
    column_ids = lax.broadcasted_iota(jnp.int32, (iface, iface), 1)

    @pl.loop(0, npair)
    def _(p):
        own = jnp.clip(pairs[0, p] - mine * owned, 0, owned - 1)
        count = counts[p]
        keep = (row_ids < count) & (column_ids < count)
        masked = jnp.where(keep, mortar[p].astype(jnp.float32), 0.0).astype(mortar.dtype)
        left[p] = lax.dot_general(
            panels[own],
            masked,
            (((0,), (0,)), ((), ())),
            preferred_element_type=jnp.float32,
        ).astype(left.dtype)

    for d in range(4):
        where_near(d, asks[d].wait_send)
    for x, way in enumerate(ways):
        for hop in range(1, len(way) - 1):
            pl.when(is_at(x, way[hop]))(passed_on(x, hop).wait_send)
    along_column = [item for item in sends if item[0] in COLUMN_STEPS]
    along_row = [item for item in sends if item[0] in ROW_STEPS]
    for d, send in along_column + along_row:
        where_near(d, send.wait_send)
    for d, send in along_column + along_row:
        where_near(d ^ 1, send.wait_recv)


def coupling_kernel(route, table, left, coupling_hbm, coupling, out_sem):
    npair, modes, _ = left.shape
    copies = []
    for p in range(npair):
        partner = table[route[p]]
        parts = FIRST_PARTS
        rows = modes // parts
        for part in range(parts):
            block = (p, pl.ds(part * rows, rows))
            coupling[block] = jnp.dot(
                left[block], partner, preferred_element_type=jnp.float32
            ).astype(coupling.dtype)
            copy = pltpu.make_async_copy(
                coupling.at[block], coupling_hbm.at[block], out_sem.at[len(copies)]
            )
            copy.start()
            copies.append(copy)
    for copy in copies:
        copy.wait()


def body(nrow, ncol, phi_modes, trace_maps, mortar, pair_list, iface_counts):
    owned, boundary, modes = phi_modes.shape
    npair, iface, _ = mortar.shape
    dtype = phi_modes.dtype
    hbm = pl.BlockSpec(memory_space=pltpu.HBM)
    smem = pl.BlockSpec(memory_space=pltpu.SMEM)
    vmem = pl.BlockSpec(memory_space=pltpu.VMEM)
    dma = pltpu.SemaphoreType.DMA
    count = len(PIECES)
    pieces = [
        pltpu.VMEM((2, CAP, extent(ROW_BLOCKS, r), extent(COLUMN_BLOCKS, c)), dtype)
        for r, c in PIECES
    ]
    table, left, route = pl.pallas_call(
        functools.partial(panels_kernel, nrow, ncol),
        out_shape=(
            pltpu.VMEM((owned + 4 * CAP, iface, modes), dtype),
            pltpu.VMEM((npair, modes, iface), dtype),
            pltpu.SMEM((npair,), jnp.int32),
        ),
        in_specs=[hbm] * 5,
        out_specs=(vmem, vmem, smem),
        scratch_shapes=[
            *[pltpu.VMEM((owned, boundary, size), dtype) for _, size in COLUMN_BLOCKS],
            *[pltpu.VMEM((owned, size, boundary), dtype) for _, size in ROW_BLOCKS],
            *pieces,
            pltpu.VMEM((2, CAP, iface, modes), dtype),
            pltpu.VMEM((owned, iface, modes), dtype),
            pltpu.VMEM((npair, iface, iface), dtype),
            pltpu.SMEM((2, npair), jnp.int32),
            pltpu.SMEM((npair,), jnp.int32),
            pltpu.SMEM((4, 128), jnp.int32),
            pltpu.SMEM((4, 128), jnp.int32),
            dma((len(COLUMN_BLOCKS), owned)),
            dma((len(ROW_BLOCKS), owned)),
            dma((3,)),
            dma((4,)),
            dma((4,)),
            dma((count, 2)),
            dma((count, 2)),
            dma((2,)),
            dma((2,)),
            pltpu.SemaphoreType.REGULAR,
            *[pltpu.VMEM((CAP, size, pieces[0].shape[3]), dtype) for _, size, _ in PASSED],
            dma((len(PASSED),)),
            dma((len(PASSED),)),
        ],
        compiler_params=pltpu.CompilerParams(
            collective_id=0, has_side_effects=True, vmem_limit_bytes=48 * 2**20
        ),
        name="panels",
    )(phi_modes, trace_maps, mortar, pair_list.T, iface_counts)
    return pl.pallas_call(
        coupling_kernel,
        out_shape=jax.ShapeDtypeStruct((npair, modes, modes), dtype),
        in_specs=[smem, vmem, vmem],
        out_specs=hbm,
        scratch_shapes=[pltpu.VMEM((npair, modes, modes), dtype), dma((npair * FIRST_PARTS,))],
        compiler_params=pltpu.CompilerParams(vmem_limit_bytes=32 * 2**20),
        name="coupling",
    )(route, table, left)


def solution(mesh):
    return jax.shard_map(
        functools.partial(body, mesh.shape["row"], mesh.shape["col"]),
        mesh=mesh,
        in_specs=(
            P(("row", "col"), None, None),
            P(("row", "col"), None, None),
            P(("row", "col"), None, None),
            P(("row", "col"), None),
            P(("row", "col")),
        ),
        out_specs=P(("row", "col"), None, None),
        check_vma=False,
    )
```
